512 devices in a mesh: rep: 16 (over y_hi, x, core), tp: 32 (over y_lo, z).
Axes of the slice: x: 4, y: 8 (y_hi: 2, y_lo: 4; y = y_hi * 4 + y_lo), z: 8, core: 2. Of those that a mesh axis runs over, the one named last changes fastest.
Arguments:
- queries: bfloat16 [2, 128, 16384], P(None, 'rep', 'tp'), may hold values from -6 to 6
- new_entries: bfloat16 [2, 2, 128, 1024], P(None, None, 'rep'), may hold values from -6 to 6
- kv_cache: bfloat16 [2, 128, 32, 1024], P(None, 'rep'), may hold values from -6 to 6
- residual: bfloat16 [2, 128, 16384], P(None, 'rep', 'tp'), may hold values from -6 to 6
- norm_gain: bfloat16 [16384], P('tp'), may hold values from 0.5 to 1.5
- serving: bfloat16 [16384, 2048], P(None, 'tp'), may hold values from -0.046875 to 0.046875
- sectioning: bfloat16 [16, 16384, 2048], P('rep', 'tp'), may hold values from -0.046875 to 0.046875
- owner_map: int32 [32], replicated, may hold values from 0 to 15, as said below
- lengths: int32 [128], P('rep'), may hold values from 1 to 32, as said below
Outputs:
- next_entries: bfloat16 [2, 128, 2048], P(None, 'rep', 'tp')
The draws below stay inside these ranges and needn't reach their ends.
Inputs may be any that keep to these rules, and one draw needn't show every extreme that they name: `owner_map`: each of the 16 replicas owns exactly 2 of the 32 row blocks. `lengths`: some row has all 32 positions valid.
All inputs are finite; a program needn't handle non-finite values.
Results may differ from the reference program's by a relative error of at most 0.008.
Values may be sent and summed in bfloat16 or wider, within the bound.
No kernel may reach another device: no remote copies, remote signals or barrier semaphores. Data moves between devices by JAX's collectives and lax.ppermute only.
A program may use at most 64 MiB of HBM per device.

```python
import jax
import jax.numpy as jnp
from jax import lax

D = 16384
KVH = 8
HD = 128
CACHE = 32
QPD = 16
ROWS = 128
N_REP = 16
N_TP = 32


def draw_owner_map(key, part):
    key = jax.random.fold_in(key, 11)
    shuffled = jax.random.permutation(key, N_TP)
    return (shuffled % N_REP).astype(jnp.int32)


def draw_lengths(key, part):
    key = jax.random.fold_in(key, 23)
    first_key, second_key = jax.random.split(key)
    drawn = jax.random.randint(first_key, (ROWS,), 1, CACHE + 1, dtype=jnp.int32)
    chosen = jax.random.randint(second_key, (), 0, ROWS, dtype=jnp.int32)
    return drawn.at[chosen].set(CACHE).astype(jnp.int32)


def level_of(own_key, extent, pieces, smallest, largest):
    factor_of, own = 1.0, jax.random.fold_in(own_key, 6)
    for position, blocks in pieces:
        heights = jnp.exp(jax.random.uniform(jax.random.fold_in(own, position), (blocks,), jnp.float32, smallest / len(pieces), largest / len(pieces)))
        factor_of = factor_of * jnp.repeat(heights, extent[position] // blocks).reshape([-1 if axis == position else 1 for axis in range(len(extent))])
    return factor_of


def normal_values(own_key, shape, width, bound, pieces=(), kind=jnp.bfloat16):
    values = width * jax.random.normal(own_key, shape, jnp.float32)
    if pieces:
        values = values * level_of(own_key, shape, pieces, -0.22, 0.18)
    return jnp.clip(values, -bound, bound).astype(kind)


def setup_inputs(seed: int = 0) -> dict:
    keys = jax.random.split(jax.random.key(seed), 10)
    queries = normal_values(keys[0], (2, ROWS, D), 1.0, 6.0, ((1, 16), (2, 32)))
    new_entries = normal_values(keys[1], (2, 2, ROWS, KVH * HD), 1.0, 6.0, ((2, 16),))
    kv_cache = normal_values(keys[2], (2, ROWS, CACHE, KVH * HD), 1.0, 6.0, ((1, 16),))
    residual = normal_values(keys[3], (2, ROWS, D), 1.0, 6.0, ((1, 16), (2, 32)))
    norm_gain = jnp.clip(1.0 + 0.1 * jax.random.normal(keys[4], (D,), jnp.float32), 0.5, 1.5).astype(jnp.bfloat16)
    serving = normal_values(keys[5], (D, 2 * KVH * HD), D ** -0.5, 0.046875, ((1, 32),))
    sectioning = normal_values(keys[6], (N_REP, D, 2 * KVH * HD), D ** -0.5, 0.046875, ((0, 16), (1, 32)))
    owner_map = draw_owner_map(jax.random.fold_in(keys[9], 71), 0)
    lengths = draw_lengths(jax.random.fold_in(keys[9], 71), 0)
    return {"queries": queries, "new_entries": new_entries, "kv_cache": kv_cache, "residual": residual, "norm_gain": norm_gain, "serving": serving, "sectioning": sectioning, "owner_map": owner_map, "lengths": lengths}


def attend_step(step_index, queries, new_entries, kv_cache, lengths):
    row_count = queries.shape[1]
    key_rows = [kv_cache[0]] + [new_entries[earlier, 0][:, None, :] for earlier in range(step_index + 1)]
    value_rows = [kv_cache[1]] + [new_entries[earlier, 1][:, None, :] for earlier in range(step_index + 1)]
    key_all = jnp.concatenate(key_rows, axis=1).astype(jnp.float32)
    value_all = jnp.concatenate(value_rows, axis=1).astype(jnp.float32)
    seq_total = key_all.shape[1]
    key_all = key_all.reshape(row_count, seq_total, KVH, HD)
    value_all = value_all.reshape(row_count, seq_total, KVH, HD)
    cached_valid = jnp.arange(CACHE, dtype=jnp.int32)[None, :] < lengths[:, None]
    valid = jnp.concatenate([cached_valid, jnp.ones((row_count, step_index + 1), dtype=bool)], axis=1)
    grouped = queries[step_index].astype(jnp.float32).reshape(row_count, KVH, QPD, HD)
    scores = jnp.einsum('rkgd,rskd->rkgs', grouped, key_all) / jnp.sqrt(jnp.float32(HD))
    scores = jnp.where(valid[:, None, None, :], scores, jnp.float32(-1e+30))
    top_score = lax.optimization_barrier(jnp.max(scores, axis=-1, keepdims=True))
    expd = jnp.exp(scores - top_score)
    weights = (expd / lax.optimization_barrier(jnp.sum(expd, axis=-1, keepdims=True))).astype(jnp.bfloat16)
    attended = jnp.einsum('rkgs,rskd->rkgd', weights.astype(jnp.float32), value_all)
    return attended.reshape(row_count, D)

def reference(queries, new_entries, kv_cache, residual, norm_gain, serving, sectioning, owner_map, lengths):
    block_rows = D // N_TP
    stacked = sectioning.reshape(N_REP, N_TP, block_rows, 2 * KVH * HD)
    fresh = stacked[owner_map, jnp.arange(N_TP, dtype=jnp.int32)].reshape(D, 2 * KVH * HD)
    outputs = []
    for step_index in range(2):
        attended = attend_step(step_index, queries, new_entries, kv_cache, lengths)
        stream = residual[step_index].astype(jnp.float32) + attended
        mean_square = lax.optimization_barrier(jnp.sum(stream * stream, axis=1, keepdims=True)) / jnp.float32(D)
        normed = (stream * jax.lax.rsqrt(mean_square + 1e-05) * norm_gain.astype(jnp.float32)).astype(jnp.bfloat16)
        weight = serving if step_index == 0 else fresh
        outputs.append(jnp.dot(normed, weight, preferred_element_type=jnp.float32).astype(jnp.bfloat16))
    return jnp.stack(outputs)
```

```python
import jax
import jax.numpy as jnp
from jax import lax
from jax.sharding import PartitionSpec as P

D = 16384
KVH = 8
HD = 128
F32 = jnp.float32
BF16 = jnp.bfloat16


def attend_local(queries_here, key_all, value_all, valid, head_width):
    row_count = queries_here.shape[0]
    head_count = queries_here.shape[1] // head_width
    grouped = queries_here.reshape(row_count, head_count, head_width)
    scores = jnp.einsum("rgd,rsd->rgs", grouped, key_all, preferred_element_type=F32)
    scores = scores / jnp.sqrt(F32(head_width))
    scores = jnp.where(valid[:, None, :], scores, F32(-1e30))
    top_score = jnp.max(scores, axis=-1, keepdims=True)
    expd = jnp.exp(scores - top_score)
    weights = (expd / jnp.sum(expd, axis=-1, keepdims=True)).astype(BF16)
    attended = jnp.einsum("rgs,rsd->rgd", weights, value_all, preferred_element_type=F32)
    return attended.reshape(row_count, head_count * head_width)


def exchange(chunks, axis):
    return lax.all_to_all(chunks, axis, split_axis=0, concat_axis=0, tiled=True)


def body(
    queries, new_entries, kv_cache, residual, norm_gain, serving, sectioning, owner_map, lengths
):
    n_rep, n_tp = lax.axis_size("rep"), lax.axis_size("tp")
    row_count, width = queries.shape[1], queries.shape[2]
    cache_span = kv_cache.shape[2]
    kv_head = lax.axis_index("tp") // (n_tp // KVH)
    cache_here = lax.dynamic_slice_in_dim(kv_cache, kv_head * HD, HD, 3)
    entries_here = lax.dynamic_slice_in_dim(new_entries, kv_head * HD, HD, 3)
    cached_valid = jnp.arange(cache_span, dtype=jnp.int32)[None, :] < lengths[:, None]
    gain_here = norm_gain.astype(F32)
    gained, squares = [], []
    for step in range(2):
        key_all, value_all = (
            jnp.concatenate(
                [cache_here[kind]] + [entries_here[e, kind][:, None, :] for e in range(step + 1)],
                axis=1,
            )
            for kind in range(2)
        )
        valid = jnp.concatenate(
            [cached_valid, jnp.ones((row_count, step + 1), dtype=bool)], axis=1
        )
        stream = residual[step].astype(F32) + attend_local(
            queries[step], key_all, value_all, valid, HD
        )
        squares.append(jnp.sum(stream * stream, axis=1))
        gained.append((stream * gain_here).astype(BF16))

    rows_all = exchange(jnp.broadcast_to(gained[1][None], (n_rep, row_count, width)), "rep")
    rows_all = rows_all.reshape(n_rep * row_count, width)
    partial = lax.dot_general(
        sectioning[0], rows_all, (((0,), (1,)), ((), ())), preferred_element_type=F32
    )
    owned = owner_map[lax.axis_index("tp")] == lax.axis_index("rep")
    partial = jnp.where(owned, partial, F32(0)).astype(BF16)
    cols = partial.shape[0] // n_tp
    partial = partial.reshape(n_tp, cols, n_rep * row_count)

    lanes = 128
    tiles = width // lanes
    features = gained[0].reshape(row_count, tiles, lanes).transpose(1, 0, 2)
    features = features.reshape(tiles * row_count, lanes)
    total = jnp.stack(squares, axis=1)
    high = total.astype(BF16)
    low = (total - high.astype(F32)).astype(BF16)
    pieces = jnp.pad(jnp.concatenate([high, low], axis=1), ((0, 8), (0, lanes - 4)))
    extra = jnp.concatenate([features, pieces], axis=0)
    message = jnp.concatenate(
        [partial, jnp.broadcast_to(extra[None], (n_tp,) + extra.shape)], axis=1
    )
    got = exchange(message, "tp")

    summed = jnp.sum(got[:, :cols, :].astype(F32), axis=0)
    mine = exchange(summed.T.astype(BF16).reshape(n_rep, row_count, cols), "rep")
    second = jnp.sum(mine.astype(F32), axis=0)

    square_parts = got[:, cols + tiles * row_count :, :4][:, :row_count, :].astype(F32)
    square_parts = jnp.sum(square_parts, axis=0)
    mean_square = (square_parts[:, :2] + square_parts[:, 2:]) / F32(D)
    scale = lax.rsqrt(mean_square + 1e-05)

    features_all = got[:, cols : cols + tiles * row_count, :]
    features_all = features_all.reshape(n_tp, tiles, row_count, lanes).transpose(2, 0, 1, 3)
    features_all = features_all.reshape(row_count, n_tp * width)
    first = jnp.dot(features_all, serving, preferred_element_type=F32)
    return jnp.stack([first * scale[:, :1], second * scale[:, 1:]]).astype(BF16)


def solution(mesh):
    placed = (
        P(None, "rep", "tp"),
        P(None, None, "rep", None),
        P(None, "rep", None, None),
        P(None, "rep", "tp"),
        P("tp"),
        P(None, "tp"),
        P("rep", "tp", None),
        P(),
        P("rep"),
    )
    return jax.shard_map(
        body, mesh=mesh, in_specs=placed, out_specs=P(None, "rep", "tp"), check_vma=False
    )
```

```python
import jax
import jax.numpy as jnp
from jax import lax
from jax.experimental import pallas as pl
from jax.experimental.pallas import tpu as pltpu
from jax.sharding import PartitionSpec as P

D = 16384
KVH = 8
HD = 128
F32 = jnp.float32
BF16 = jnp.bfloat16
NT = (((1,), (1,)), ((), ()))


def exchange(chunks, axis, groups=None):
    return lax.all_to_all(
        chunks, axis, split_axis=0, concat_axis=0, axis_index_groups=groups, tiled=True
    )


def attend_kernel(head_ref, lengths_ref, q_ref, e_ref, kv_ref, res_ref, gain_ref, send_ref, extra_ref):
    rows, span = kv_ref.shape[1], kv_ref.shape[2]
    tiles = q_ref.shape[2] // HD
    cached = rows * span
    n_keys = cached + 2 * rows
    n_queries = 2 * tiles * rows

    def stacked(value):
        return jnp.concatenate([value[:, t * HD : (t + 1) * HD] for t in range(tiles)], axis=0)

    query = jnp.concatenate([stacked(q_ref[s].astype(F32)) for s in range(2)], axis=0).astype(BF16)

    def keys(kind):
        fresh = jnp.concatenate([e_ref[s, kind].astype(F32) for s in range(2)], axis=0)
        return jnp.concatenate([kv_ref[kind].reshape(cached, HD), fresh.astype(BF16)], axis=0)

    scores = lax.dot_general(query, keys(0), NT, preferred_element_type=F32)
    scores = scores / jnp.sqrt(F32(HD))
    column = lax.broadcasted_iota(jnp.int32, (n_queries, n_keys), 1)
    line = lax.broadcasted_iota(jnp.int32, (n_queries, n_keys), 0)
    old = column < cached
    row_of_key = jnp.where(old, lax.div(column, span), lax.rem(column, rows))
    limit = jnp.zeros_like(column)
    for r in range(rows):
        limit = jnp.where(row_of_key == r, lengths_ref[r], limit)
    late = jnp.where(column < cached + rows, 0, tiles * rows)
    bar = jnp.where(old, lax.rem(column, span), late)
    against = jnp.where(old, limit - 1, line)
    seen = (bar <= against) & (row_of_key == lax.rem(line, rows))
    scores = jnp.where(seen, scores, F32(-1e30))
    top = jnp.max(scores, axis=1, keepdims=True)
    expd = jnp.exp(scores - top)
    weights = (expd / jnp.sum(expd, axis=1, keepdims=True)).astype(BF16)
    attended = jnp.dot(weights, keys(1), preferred_element_type=F32)

    lane = lax.broadcasted_iota(jnp.int32, (rows, HD), 1)
    pieces = jnp.zeros((rows, HD), F32)
    gain = gain_ref[...].astype(F32)
    for s in range(2):
        base = s * tiles * rows
        there = jnp.concatenate(
            [attended[base + t * rows : base + (t + 1) * rows] for t in range(tiles)], axis=1
        )
        stream = res_ref[s].astype(F32) + there
        square = jnp.sum(stream * stream, axis=1, keepdims=True)
        high = square.astype(BF16).astype(F32)
        pieces = jnp.where(lane == s, high, jnp.where(lane == 2 + s, square - high, pieces))
        gained = stream * gain
        if s == 0:
            first = stacked(gained)
        else:
            gained = gained.astype(BF16)
            for p in range(send_ref.shape[0]):
                send_ref[p] = gained
    extra_ref[...] = jnp.concatenate([first, pieces], axis=0).astype(BF16)


def product_kernel(pick_ref, rows_ref, mine_ref, peer_ref, extra_ref, out_ref):
    n_tp = out_ref.shape[0]
    cols = mine_ref.shape[2] // n_tp
    chips, per, width = rows_ref.shape
    count = chips * per
    half = count // 2
    low = lax.broadcasted_iota(jnp.int32, (half, 2 * cols), 1) < cols
    extra = extra_ref[...].astype(F32)

    def fill(weight_ref):
        rows = rows_ref[...].astype(F32).reshape(count, width).astype(BF16)
        step = 512
        for start in range(0, n_tp * cols, step):
            part = jnp.dot(
                rows, weight_ref[0, :, start : start + step], preferred_element_type=F32
            )
            for j in range(step // (2 * cols)):
                tile = part[:, j * 2 * cols : (j + 1) * 2 * cols]
                turned = pltpu.roll(tile, cols, 1)
                even = jnp.where(low, tile[:half], turned[half:])
                odd = jnp.where(low, turned[:half], tile[half:])
                at = start // cols + 2 * j
                out_ref[at] = jnp.concatenate([even, extra], axis=0).astype(BF16)
                out_ref[at + 1] = jnp.concatenate([odd, extra], axis=0).astype(BF16)

    pick = pick_ref[0]

    @pl.when(pick == 0)
    def _():
        fill(mine_ref)

    @pl.when(pick == 1)
    def _():
        fill(peer_ref)

    @pl.when(pick > 1)
    def _():
        empty = jnp.concatenate([jnp.zeros((half, 2 * cols), F32), extra], axis=0).astype(BF16)
        for at in range(n_tp):
            out_ref[at] = empty


def attend(head, lengths, queries, entries, cache, residual, gain, n_chips):
    _, rows, width = queries.shape
    span = cache.shape[2]
    tiles = width // HD
    whole = lambda *shape: pl.BlockSpec(shape, lambda i, *_: (0,) * len(shape))
    by_head = lambda *shape: pl.BlockSpec(
        shape, lambda i, head_ref, _: (0,) * (len(shape) - 1) + (head_ref[0],)
    )
    return pl.pallas_call(
        attend_kernel,
        grid_spec=pltpu.PrefetchScalarGridSpec(
            num_scalar_prefetch=2,
            grid=(1,),
            in_specs=[
                whole(2, rows, width),
                by_head(2, 2, rows, HD),
                by_head(2, rows, span, HD),
                whole(2, rows, width),
                whole(1, width),
            ],
            out_specs=[whole(n_chips, rows, width), whole((tiles + 1) * rows, HD)],
        ),
        out_shape=[
            jax.ShapeDtypeStruct((n_chips, rows, width), BF16),
            jax.ShapeDtypeStruct(((tiles + 1) * rows, HD), BF16),
        ],
        compiler_params=pltpu.CompilerParams(vmem_limit_bytes=16 * 2**20),
        cost_estimate=pl.CostEstimate(flops=10**7, bytes_accessed=300_000, transcendentals=20_000),
    )(head, lengths, queries, entries, cache, residual, gain)


def product(pick, rows_all, mine, peer, extra, n_tp):
    vmem = pl.BlockSpec(memory_space=pltpu.VMEM)
    chips, per, _ = rows_all.shape
    cols = mine.shape[2] // n_tp
    lines = chips * per // 2 + extra.shape[0]
    return pl.pallas_call(
        product_kernel,
        in_specs=[pl.BlockSpec(memory_space=pltpu.SMEM), vmem, vmem, vmem, vmem],
        out_specs=vmem,
        out_shape=jax.ShapeDtypeStruct((n_tp, lines, 2 * cols), BF16),
        compiler_params=pltpu.CompilerParams(vmem_limit_bytes=16 * 2**20),
        cost_estimate=pl.CostEstimate(flops=13 * 10**7, bytes_accessed=3_000_000, transcendentals=0),
    )(pick, rows_all, mine, peer, extra)


def body(
    queries, new_entries, kv_cache, residual, norm_gain, serving, sectioning, owner_map, lengths
):
    n_rep, n_tp = lax.axis_size("rep"), lax.axis_size("tp")
    n_chips = n_rep // 2
    row_count, width = queries.shape[1], queries.shape[2]
    rep, tp = lax.axis_index("rep"), lax.axis_index("tp")
    kv_head = (tp // (n_tp // KVH)).astype(jnp.int32).reshape(1)
    send, extra = attend(
        kv_head, lengths, queries, new_entries, kv_cache, residual, norm_gain[None], n_chips
    )

    same_core = [[i for i in range(n_rep) if i % 2 == core] for core in range(2)]
    rows_all = exchange(send, "rep", same_core)
    peer_rows = lax.ppermute(sectioning, "rep", [(i, i ^ 1) for i in range(n_rep)])
    owner = owner_map[tp]
    pick = jnp.where(owner == rep, 0, jnp.where(owner == (rep ^ 1), 1, 2))
    message = product(
        pick.astype(jnp.int32).reshape(1), rows_all, sectioning, peer_rows, extra, n_tp
    )

    half = n_chips * row_count // 2
    tiles = width // HD
    got = exchange(message, "tp")
    cols = sectioning.shape[2] // n_tp
    summed = jnp.sum(got[:, :half].astype(F32), axis=0).astype(BF16)
    summed = summed.reshape(n_chips // 2, row_count, 2 * cols)
    mine = exchange(jnp.concatenate([summed, summed], axis=0), "rep", same_core)
    second = jnp.sum(mine.astype(F32), axis=0)
    second = jnp.where(rep // 2 < n_chips // 2, second[:, :cols], second[:, cols:])

    parts = jnp.sum(got[:, half + tiles * row_count :, :4].astype(F32), axis=0)
    mean_square = (parts[:, :2] + parts[:, 2:]) / F32(D)
    scale = lax.rsqrt(mean_square + 1e-05)
    features = got[:, half : half + tiles * row_count].reshape(n_tp, tiles, row_count, HD)
    features = features.transpose(2, 0, 1, 3).reshape(row_count, n_tp * width)
    first = jnp.dot(features, serving, preferred_element_type=F32)
    return jnp.stack([first * scale[:, :1], second * scale[:, 1:]]).astype(BF16)


def solution(mesh):
    placed = (
        P(None, "rep", "tp"),
        P(None, None, "rep", None),
        P(None, "rep", None, None),
        P(None, "rep", "tp"),
        P("tp"),
        P(None, "tp"),
        P("rep", "tp", None),
        P(),
        P("rep"),
    )
    return jax.shard_map(
        body, mesh=mesh, in_specs=placed, out_specs=P(None, "rep", "tp"), check_vma=False
    )
```

```python
import jax
import jax.numpy as jnp
from jax import lax
from jax.experimental import pallas as pl
from jax.experimental.pallas import tpu as pltpu
from jax.sharding import PartitionSpec as P

D = 16384
KVH = 8
HD = 128
F32 = jnp.float32
BF16 = jnp.bfloat16
NT = (((1,), (1,)), ((), ()))


def exchange(chunks, axis, groups=None):
    return lax.all_to_all(
        chunks, axis, split_axis=0, concat_axis=0, axis_index_groups=groups, tiled=True
    )


def attend_kernel(
    lengths_hbm, q_hbm, e_hbm, kv_hbm, res_hbm, gain_hbm, send_ref, extra_ref,
    lengths_ref, q_ref, e_ref, kv_ref, res_ref, gain_ref, sems,
):
    head = lax.div(lax.axis_index("tp"), lax.div(lax.axis_size("tp"), KVH))
    columns = pl.ds(pl.multiple_of(head * HD, HD), HD)
    copies = [
        pltpu.make_async_copy(source, target, sems.at[i])
        for i, (source, target) in enumerate(
            [
                (kv_hbm.at[:, :, :, columns], kv_ref),
                (e_hbm.at[:, :, :, columns], e_ref),
                (q_hbm, q_ref),
                (lengths_hbm, lengths_ref),
                (res_hbm, res_ref),
                (gain_hbm, gain_ref),
            ]
        )
    ]
    for copy in copies:
        copy.start()
    rows, span = kv_ref.shape[1], kv_ref.shape[2]
    tiles = q_ref.shape[2] // HD
    cached = rows * span
    n_keys = cached + 2 * rows
    n_queries = 2 * tiles * rows

    def stacked(value):
        return jnp.concatenate([value[:, t * HD : (t + 1) * HD] for t in range(tiles)], axis=0)

    def keys(kind):
        fresh = jnp.concatenate([e_ref[s, kind].astype(F32) for s in range(2)], axis=0)
        return jnp.concatenate([kv_ref[kind].reshape(cached, HD), fresh.astype(BF16)], axis=0)

    column = lax.broadcasted_iota(jnp.int32, (n_queries, n_keys), 1)
    line = lax.broadcasted_iota(jnp.int32, (n_queries, n_keys), 0)
    old = column < cached
    row_of_key = jnp.where(old, lax.div(column, span), lax.rem(column, rows))
    for copy in copies:
        copy.wait()
    query = jnp.concatenate([stacked(q_ref[s].astype(F32)) for s in range(2)], axis=0).astype(BF16)
    scores = lax.dot_general(query, keys(0), NT, preferred_element_type=F32)
    scores = scores / jnp.sqrt(F32(HD))
    limit = jnp.zeros_like(column)
    for r in range(rows):
        limit = jnp.where(row_of_key == r, lengths_ref[r], limit)
    late = jnp.where(column < cached + rows, 0, tiles * rows)
    bar = jnp.where(old, lax.rem(column, span), late)
    against = jnp.where(old, limit - 1, line)
    seen = (bar <= against) & (row_of_key == lax.rem(line, rows))
    scores = jnp.where(seen, scores, F32(-1e30))
    top = jnp.max(scores, axis=1, keepdims=True)
    expd = jnp.exp(scores - top)
    weights = (expd / jnp.sum(expd, axis=1, keepdims=True)).astype(BF16)
    attended = jnp.dot(weights, keys(1), preferred_element_type=F32)

    lane = lax.broadcasted_iota(jnp.int32, (rows, HD), 1)
    pieces = jnp.zeros((rows, HD), F32)
    gain = gain_ref[...].astype(F32)[None]
    for s in range(2):
        base = s * tiles * rows
        there = jnp.concatenate(
            [attended[base + t * rows : base + (t + 1) * rows] for t in range(tiles)], axis=1
        )
        stream = res_ref[s].astype(F32) + there
        square = jnp.sum(stream * stream, axis=1, keepdims=True)
        high = square.astype(BF16).astype(F32)
        pieces = jnp.where(lane == s, high, jnp.where(lane == 2 + s, square - high, pieces))
        gained = stream * gain
        if s == 0:
            first = stacked(gained)
        else:
            gained = gained.astype(BF16)
            for p in range(send_ref.shape[0]):
                send_ref[p] = gained
    extra_ref[...] = jnp.concatenate([first, pieces], axis=0).astype(BF16)


def product_kernel(
    pick_ref, rows_hbm, mine_hbm, peer_hbm, extra_hbm, out_hbm,
    rows_ref, extra_ref, weight_ref, out_ref, in_sems, out_sems,
):
    n_tp = out_ref.shape[0]
    cols = mine_hbm.shape[2] // n_tp
    chips, per, width = rows_ref.shape
    count = chips * per
    half = count // 2
    n_steps, _, step = weight_ref.shape
    each = n_tp // n_steps
    pick = pick_ref[0]

    def fetch(source, i):
        return pltpu.make_async_copy(
            source.at[0, :, pl.ds(i * step, step)], weight_ref.at[i], in_sems.at[i]
        )

    def ship(i):
        part = pl.ds(i * each, each)
        return pltpu.make_async_copy(out_ref.at[part], out_hbm.at[part], out_sems.at[i])

    small = [
        pltpu.make_async_copy(extra_hbm, extra_ref, in_sems.at[n_steps]),
        pltpu.make_async_copy(rows_hbm, rows_ref, in_sems.at[n_steps + 1]),
    ]
    for copy in small:
        copy.start()

    @pl.when(pick == 0)
    def _():
        for i in range(n_steps):
            fetch(mine_hbm, i).start()

    @pl.when(pick == 1)
    def _():
        for i in range(n_steps):
            fetch(peer_hbm, i).start()

    for copy in small:
        copy.wait()
    extra = extra_ref[...].astype(F32)

    @pl.when(pick < 2)
    def _():
        low = lax.broadcasted_iota(jnp.int32, (half, 2 * cols), 1) < cols
        rows = rows_ref[...].reshape(count, width)

        def one(i, carry):
            fetch(mine_hbm, i).wait()
            part = jnp.dot(rows, weight_ref[i], preferred_element_type=F32)
            for j in range(each // 2):
                tile = part[:, j * 2 * cols : (j + 1) * 2 * cols]
                turned = pltpu.roll(tile, cols, 1)
                even = jnp.where(low, tile[:half], turned[half:])
                odd = jnp.where(low, turned[:half], tile[half:])
                at = i * each + 2 * j
                out_ref[at] = jnp.concatenate([even, extra], axis=0).astype(BF16)
                out_ref[at + 1] = jnp.concatenate([odd, extra], axis=0).astype(BF16)
            ship(i).start()
            return carry

        lax.fori_loop(0, n_steps, one, 0)

    @pl.when(pick > 1)
    def _():
        empty = jnp.concatenate([jnp.zeros((half, 2 * cols), F32), extra], axis=0).astype(BF16)

        def one(at, carry):
            out_ref[at] = empty
            return carry

        lax.fori_loop(0, n_tp, one, 0)
        for i in range(n_steps):
            ship(i).start()

    for i in range(n_steps):
        ship(i).wait()


VMEM_SPEC = pl.BlockSpec(memory_space=pltpu.VMEM)
HBM_SPEC = pl.BlockSpec(memory_space=pltpu.HBM)
ANY_SPEC = pl.BlockSpec(memory_space=pl.ANY)


def attend(lengths, queries, entries, cache, residual, gain, n_chips):
    _, rows, width = queries.shape
    span = cache.shape[2]
    tiles = width // HD
    return pl.pallas_call(
        attend_kernel,
        in_specs=[HBM_SPEC] * 6,
        out_specs=[VMEM_SPEC] * 2,
        out_shape=[
            jax.ShapeDtypeStruct((n_chips, rows, width), BF16),
            jax.ShapeDtypeStruct(((tiles + 1) * rows, HD), BF16),
        ],
        scratch_shapes=[
            pltpu.SMEM((rows,), jnp.int32),
            pltpu.VMEM((2, rows, width), BF16),
            pltpu.VMEM((2, 2, rows, HD), BF16),
            pltpu.VMEM((2, rows, span, HD), BF16),
            pltpu.VMEM((2, rows, width), BF16),
            pltpu.VMEM((width,), BF16),
            pltpu.SemaphoreType.DMA((6,)),
        ],
        compiler_params=pltpu.CompilerParams(vmem_limit_bytes=60 * 2**20),
        cost_estimate=pl.CostEstimate(flops=10**7, bytes_accessed=300_000, transcendentals=20_000),
    )(lengths, queries, entries, cache, residual, gain)


def product(pick, rows_all, mine, peer, extra, n_tp):
    chips, per, width = rows_all.shape
    cols = mine.shape[2] // n_tp
    message = (n_tp, chips * per // 2 + extra.shape[0], 2 * cols)
    step = 16 * cols
    n_steps = n_tp * cols // step
    return pl.pallas_call(
        product_kernel,
        in_specs=[pl.BlockSpec(memory_space=pltpu.SMEM), ANY_SPEC, HBM_SPEC, HBM_SPEC, ANY_SPEC],
        out_specs=HBM_SPEC,
        out_shape=jax.ShapeDtypeStruct(message, BF16),
        scratch_shapes=[
            pltpu.VMEM(rows_all.shape, BF16),
            pltpu.VMEM(extra.shape, BF16),
            pltpu.VMEM((n_steps, width, step), BF16),
            pltpu.VMEM(message, BF16),
            pltpu.SemaphoreType.DMA((n_steps + 2,)),
            pltpu.SemaphoreType.DMA((n_steps,)),
        ],
        compiler_params=pltpu.CompilerParams(vmem_limit_bytes=60 * 2**20),
        cost_estimate=pl.CostEstimate(flops=13 * 10**7, bytes_accessed=3_000_000, transcendentals=0),
    )(pick, rows_all, mine, peer, extra)


def body(
    queries, new_entries, kv_cache, residual, norm_gain, serving, sectioning, owner_map, lengths
):
    n_rep, n_tp = lax.axis_size("rep"), lax.axis_size("tp")
    n_chips = n_rep // 2
    row_count, width = queries.shape[1], queries.shape[2]
    rep, tp = lax.axis_index("rep"), lax.axis_index("tp")
    send, extra = attend(
        lengths, queries, new_entries, kv_cache, residual, norm_gain, n_chips
    )
    sectioning, send = lax.optimization_barrier((sectioning, send))

    same_core = [[i for i in range(n_rep) if i % 2 == core] for core in range(2)]
    rows_all = exchange(send, "rep", same_core)
    peer_rows = lax.ppermute(sectioning, "rep", [(i, i ^ 1) for i in range(n_rep)])
    owner = owner_map[tp]
    pick = jnp.where(owner == rep, 0, jnp.where(owner == (rep ^ 1), 1, 2))
    message = product(
        pick.astype(jnp.int32).reshape(1), rows_all, sectioning, peer_rows, extra, n_tp
    )

    half = n_chips * row_count // 2
    tiles = width // HD
    got = exchange(message, "tp")
    cols = sectioning.shape[2] // n_tp
    summed = jnp.sum(got[:, :half].astype(F32), axis=0).astype(BF16)
    summed = summed.reshape(n_chips // 2, row_count, 2 * cols)
    mine = exchange(jnp.concatenate([summed, summed], axis=0), "rep", same_core)
    second = jnp.sum(mine.astype(F32), axis=0)
    second = jnp.where(rep // 2 < n_chips // 2, second[:, :cols], second[:, cols:])

    parts = jnp.sum(got[:, half + tiles * row_count :, :4].astype(F32), axis=0)
    mean_square = (parts[:, :2] + parts[:, 2:]) / F32(D)
    scale = lax.rsqrt(mean_square + 1e-05)
    features = got[:, half : half + tiles * row_count].reshape(n_tp, tiles, row_count, HD)
    features = features.transpose(2, 0, 1, 3).reshape(row_count, n_tp * width)
    first = jnp.dot(features, serving, preferred_element_type=F32)
    return jnp.stack([first * scale[:, :1], second * scale[:, 1:]]).astype(BF16)


def solution(mesh):
    placed = (
        P(None, "rep", "tp"),
        P(None, None, "rep", None),
        P(None, "rep", None, None),
        P(None, "rep", "tp"),
        P("tp"),
        P(None, "tp"),
        P("rep", "tp", None),
        P(),
        P("rep"),
    )
    return jax.shard_map(
        body, mesh=mesh, in_specs=placed, out_specs=P(None, "rep", "tp"), check_vma=False
    )
```

```python
import jax
import jax.numpy as jnp
from jax import lax
from jax.experimental import pallas as pl
from jax.experimental.pallas import tpu as pltpu
from jax.sharding import PartitionSpec as P

D = 16384
KVH = 8
HD = 128
F32 = jnp.float32
BF16 = jnp.bfloat16
NT = (((1,), (1,)), ((), ()))


def exchange(chunks, axis, groups=None):
    return lax.all_to_all(
        chunks, axis, split_axis=0, concat_axis=0, axis_index_groups=groups, tiled=True
    )


def attend_kernel(
    lengths_hbm, q_hbm, e_hbm, kv_hbm, res_hbm, gain_hbm, send_ref,
    lengths_ref, q_ref, e_ref, kv_ref, res_ref, gain_ref, sems,
):
    head = lax.div(lax.axis_index("tp"), lax.div(lax.axis_size("tp"), KVH))
    columns = pl.ds(pl.multiple_of(head * HD, HD), HD)
    copies = [
        pltpu.make_async_copy(source, target, sems.at[i])
        for i, (source, target) in enumerate(
            [
                (kv_hbm.at[:, :, :, columns], kv_ref),
                (e_hbm.at[:, :, :, columns], e_ref),
                (q_hbm, q_ref),
                (lengths_hbm, lengths_ref),
                (res_hbm, res_ref),
                (gain_hbm, gain_ref),
            ]
        )
    ]
    for copy in copies:
        copy.start()
    rows, span = kv_ref.shape[1], kv_ref.shape[2]
    tiles = q_ref.shape[2] // HD
    cached = rows * span
    n_keys = cached + 2 * rows
    n_queries = 2 * tiles * rows

    def stacked(value):
        return jnp.concatenate([value[:, t * HD : (t + 1) * HD] for t in range(tiles)], axis=0)

    def keys(kind):
        fresh = jnp.concatenate([e_ref[s, kind].astype(F32) for s in range(2)], axis=0)
        return jnp.concatenate([kv_ref[kind].reshape(cached, HD), fresh.astype(BF16)], axis=0)

    column = lax.broadcasted_iota(jnp.int32, (n_queries, n_keys), 1)
    line = lax.broadcasted_iota(jnp.int32, (n_queries, n_keys), 0)
    old = column < cached
    row_of_key = jnp.where(old, lax.div(column, span), lax.rem(column, rows))
    for copy in copies:
        copy.wait()
    query = jnp.concatenate([stacked(q_ref[s].astype(F32)) for s in range(2)], axis=0).astype(BF16)
    scores = lax.dot_general(query, keys(0), NT, preferred_element_type=F32)
    scores = scores / jnp.sqrt(F32(HD))
    limit = jnp.zeros_like(column)
    for r in range(rows):
        limit = jnp.where(row_of_key == r, lengths_ref[r], limit)
    late = jnp.where(column < cached + rows, 0, tiles * rows)
    bar = jnp.where(old, lax.rem(column, span), late)
    against = jnp.where(old, limit - 1, line)
    seen = (bar <= against) & (row_of_key == lax.rem(line, rows))
    scores = jnp.where(seen, scores, F32(-1e30))
    top = jnp.max(scores, axis=1, keepdims=True)
    expd = jnp.exp(scores - top)
    weights = (expd / jnp.sum(expd, axis=1, keepdims=True)).astype(BF16)
    attended = jnp.dot(weights, keys(1), preferred_element_type=F32)

    lane = lax.broadcasted_iota(jnp.int32, (rows, HD), 1)
    gain = gain_ref[...].astype(F32)[None]
    gained, squares = [], []
    for s in range(2):
        base = s * tiles * rows
        there = jnp.concatenate(
            [attended[base + t * rows : base + (t + 1) * rows] for t in range(tiles)], axis=1
        )
        stream = res_ref[s].astype(F32) + there
        squares.append(jnp.sum(stream * stream, axis=1, keepdims=True))
        gained.append(stream * gain)
    spot = lane % (HD // 2)
    pieces = jnp.zeros((rows, HD), F32)
    for s in range(2):
        high = squares[s].astype(BF16).astype(F32)
        pieces = jnp.where(
            spot == s, high, jnp.where(spot == 2 + s, squares[s] - high, pieces)
        )
    second = gained[1].astype(BF16)
    for p in range(send_ref.shape[0]):
        tile = gained[0][:, p // 2 * HD : (p // 2 + 1) * HD]
        own = (lane >= HD // 2) if p % 2 else (lane < HD // 2)
        send_ref[p, :, : tiles * HD] = second
        send_ref[p, :, tiles * HD :] = jnp.where(own, tile, pieces).astype(BF16)


def product_kernel(
    pick_ref, rows_hbm, mine_hbm, peer_hbm, out_hbm,
    rows_ref, weight_ref, out_ref, in_sems, out_sems,
):
    n_tp, chips, per, _ = out_ref.shape
    cols = mine_hbm.shape[2] // n_tp
    n_steps, width, step = weight_ref.shape
    count = chips * per
    each = n_tp // n_steps
    pick = pick_ref[0]

    def fetch(source, i):
        return pltpu.make_async_copy(
            source.at[0, :, pl.ds(i * step, step)], weight_ref.at[i], in_sems.at[i]
        )

    def ship(i):
        part = pl.ds(i * each, each)
        return pltpu.make_async_copy(out_ref.at[part], out_hbm.at[part], out_sems.at[i])

    small = pltpu.make_async_copy(rows_hbm, rows_ref, in_sems.at[n_steps])
    small.start()

    @pl.when(pick == 0)
    def _():
        for i in range(n_steps):
            fetch(mine_hbm, i).start()

    @pl.when(pick == 1)
    def _():
        for i in range(n_steps):
            fetch(peer_hbm, i).start()

    small.wait()

    @pl.when(pick < 2)
    def _():
        rows = rows_ref[:, :, :width].reshape(count, width)
        other = rows_ref[:, :, width:].astype(F32).reshape(count, 2 * cols)
        right = lax.broadcasted_iota(jnp.int32, (count, 2 * cols), 1) >= cols
        odd_place = lax.rem(lax.div(lax.axis_index("rep"), 2), 2) == 1
        odd_lanes = jnp.full((count, 2 * cols), jnp.where(odd_place, 1, 0)) == 1
        features = jnp.where(right, 1, 0) == jnp.where(odd_place, 1, 0)

        def one(i, carry):
            fetch(mine_hbm, i).wait()
            part = jnp.dot(rows, weight_ref[i], preferred_element_type=F32)
            for j in range(each // 2):
                tile = part[:, j * 2 * cols : (j + 1) * 2 * cols]
                turned = pltpu.roll(tile, cols, 1)
                left_block = jnp.where(odd_lanes, tile, turned)
                right_block = jnp.where(odd_lanes, turned, tile)
                at = i * each + 2 * j
                for k, block in enumerate((left_block, right_block)):
                    block = jnp.where(features, other, block)
                    out_ref[at + k] = block.reshape(chips, per, 2 * cols).astype(BF16)
            ship(i).start()
            return carry

        lax.fori_loop(0, n_steps, one, 0)

    @pl.when(pick > 1)
    def _():
        same = rows_ref[:, :, width:]

        def one(at, carry):
            out_ref[at] = same
            return carry

        lax.fori_loop(0, n_tp, one, 0)
        for i in range(n_steps):
            ship(i).start()

    for i in range(n_steps):
        ship(i).wait()


VMEM_SPEC = pl.BlockSpec(memory_space=pltpu.VMEM)
HBM_SPEC = pl.BlockSpec(memory_space=pltpu.HBM)
ANY_SPEC = pl.BlockSpec(memory_space=pl.ANY)


def attend(lengths, queries, entries, cache, residual, gain, n_chips):
    _, rows, width = queries.shape
    span = cache.shape[2]
    return pl.pallas_call(
        attend_kernel,
        in_specs=[HBM_SPEC] * 6,
        out_specs=VMEM_SPEC,
        out_shape=jax.ShapeDtypeStruct((n_chips, rows, width + HD), BF16),
        scratch_shapes=[
            pltpu.SMEM((rows,), jnp.int32),
            pltpu.VMEM((2, rows, width), BF16),
            pltpu.VMEM((2, 2, rows, HD), BF16),
            pltpu.VMEM((2, rows, span, HD), BF16),
            pltpu.VMEM((2, rows, width), BF16),
            pltpu.VMEM((width,), BF16),
            pltpu.SemaphoreType.DMA((6,)),
        ],
        compiler_params=pltpu.CompilerParams(vmem_limit_bytes=60 * 2**20),
        cost_estimate=pl.CostEstimate(flops=10**7, bytes_accessed=300_000, transcendentals=20_000),
    )(lengths, queries, entries, cache, residual, gain)


def product(pick, rows_all, mine, peer, n_tp):
    chips, per, _ = rows_all.shape
    width = mine.shape[1]
    cols = mine.shape[2] // n_tp
    message = (n_tp, chips, per, 2 * cols)
    step = 16 * cols
    n_steps = n_tp * cols // step
    return pl.pallas_call(
        product_kernel,
        in_specs=[pl.BlockSpec(memory_space=pltpu.SMEM), ANY_SPEC, HBM_SPEC, HBM_SPEC],
        out_specs=HBM_SPEC,
        out_shape=jax.ShapeDtypeStruct(message, BF16),
        scratch_shapes=[
            pltpu.VMEM(rows_all.shape, BF16),
            pltpu.VMEM((n_steps, width, step), BF16),
            pltpu.VMEM(message, BF16),
            pltpu.SemaphoreType.DMA((n_steps + 1,)),
            pltpu.SemaphoreType.DMA((n_steps,)),
        ],
        compiler_params=pltpu.CompilerParams(vmem_limit_bytes=60 * 2**20),
        cost_estimate=pl.CostEstimate(flops=13 * 10**7, bytes_accessed=3_000_000, transcendentals=0),
    )(pick, rows_all, mine, peer)


def body(
    queries, new_entries, kv_cache, residual, norm_gain, serving, sectioning, owner_map, lengths
):
    n_rep, n_tp = lax.axis_size("rep"), lax.axis_size("tp")
    n_chips = n_rep // 2
    row_count, width = queries.shape[1], queries.shape[2]
    cols = serving.shape[1]
    rep, tp = lax.axis_index("rep"), lax.axis_index("tp")
    send = attend(lengths, queries, new_entries, kv_cache, residual, norm_gain, n_chips)
    sectioning, send = lax.optimization_barrier((sectioning, send))

    same_core = [[i for i in range(n_rep) if i % 2 == core] for core in range(2)]
    rows_all = exchange(send, "rep", same_core)
    peer_rows = lax.ppermute(sectioning, "rep", [(i, i ^ 1) for i in range(n_rep)])
    owner = owner_map[tp]
    pick = jnp.where(owner == rep, 0, jnp.where(owner == (rep ^ 1), 1, 2))
    message = product(pick.astype(jnp.int32).reshape(1), rows_all, sectioning, peer_rows, n_tp)

    everyone = [[r * n_tp + t for t in range(n_tp) for r in replicas] for replicas in same_core]
    got = exchange(
        message.reshape(n_tp * n_chips, row_count, 2 * cols), ("rep", "tp"), everyone
    ).reshape(n_tp, n_chips // 2, 2, row_count, 2 * cols)
    left = jnp.arange(2 * cols, dtype=jnp.int32)[None, None, None, :] < cols
    features = jnp.where(left, got[:, :, 0], got[:, :, 1])
    features = features.transpose(2, 0, 1, 3).reshape(row_count, n_tp * width)
    first = jnp.dot(features, serving, preferred_element_type=F32)

    mixed = jnp.where(left, got[:, :, 1], got[:, :, 0]).astype(F32)
    pair = jnp.arange(n_chips // 2, dtype=jnp.int32)[None, :, None, None]
    source = 2 * pair + jnp.where(left, 1, 0)
    chip = (owner_map // 2)[:, None, None, None]
    second = jnp.sum(jnp.where(chip == source, mixed, F32(0)), axis=(0, 1))
    second = second[:, :cols] + second[:, cols:]
    squares = jnp.sum(jnp.where((chip ^ 1) == source, mixed, F32(0)), axis=(0, 1))
    squares = squares[:, :cols] + squares[:, cols:]
    mean_square = (squares[:, :2] + squares[:, 2:4]) / F32(D)
    scale = lax.rsqrt(mean_square + 1e-05)
    return jnp.stack([first * scale[:, :1], second * scale[:, 1:]]).astype(BF16)


def solution(mesh):
    placed = (
        P(None, "rep", "tp"),
        P(None, None, "rep", None),
        P(None, "rep", None, None),
        P(None, "rep", "tp"),
        P("tp"),
        P(None, "tp"),
        P("rep", "tp", None),
        P(),
        P("rep"),
    )
    return jax.shard_map(
        body, mesh=mesh, in_specs=placed, out_specs=P(None, "rep", "tp"), check_vma=False
    )
```
